32 devices in a mesh: groups: 2 (over y), leaf: 4 (over z), near: 2 (over x), rhs: 2 (over core).
Axes of the slice: x: 2, y: 2, z: 4, core: 2. Of those that a mesh axis runs over, the one named last changes fastest.
Arguments:
- points: bfloat16 [3, 256, 1024], P(None, None, ('groups', 'leaf')), parts along dimension 2, may hold values from -24 to 24, as said below
- charges: bfloat16 [256, 64, 1024], P('near', 'rhs', ('groups', 'leaf')), parts along dimension 2, may hold values from -6 to 6
- basis: bfloat16 [256, 64, 1024], P('near', None, ('groups', 'leaf')), parts along dimension 2, may hold values from -0.375 to 0.375
- transfer: bfloat16 [64, 64, 1024], P(None, None, ('groups', 'leaf')), parts along dimension 2, may hold values from -0.25 to 0.25
- leaf_skeleton: bfloat16 [3, 64, 1024], P(None, None, ('groups', 'leaf')), parts along dimension 2, may hold values from -2 to 2
- parent_skeleton: bfloat16 [3, 64, 128], P(None, None, ('groups', 'leaf')), parts along dimension 2, may hold values from -2 to 2
- near_list: int32 [25, 1024], P(None, ('groups', 'leaf')), parts along dimension 1, may hold values from 0 to 511, as said below
- near_count: int32 [1024], P(('groups', 'leaf')), parts along dimension 0, may hold values from 1 to 25
- leaf_far: int32 [16, 1024], P(None, ('groups', 'leaf')), parts along dimension 1, may hold values from 0 to 511, as said below
- parent_far: int32 [16, 128], P(None, ('groups', 'leaf')), parts along dimension 1, may hold values from 0 to 63, as said below
Outputs:
- potential: bfloat16 [256, 64, 1024], P('near', 'rhs', ('groups', 'leaf')), parts along dimension 2
The draws below stay inside these ranges and needn't reach their ends.
There are 2 independent parts, one for each index of `groups`. The reference program is written for one: setup_inputs(seed, part) draws one part's arguments, and reference() takes and returns one part's arrays. A program takes and returns all parts, laid end to end along the dimension named above; each array names one. Nothing has to cross between parts.
Inputs may be any that keep to these rules, and one draw needn't show every extreme that they name: `points`: offsets of an element from its leaf's centre; the third component lies within 2 of zero. `near_list`: slot 0 of leaf i is i; the other live slots name distinct leaves whose strip positions (i mod 8, floor(i / 8)) differ from i's by at most 2 in each coordinate; slots from near_count[i] on hold i. `leaf_far`: entry of leaf i names a leaf that is not in i's 5 by 5 near block and whose strip row floor(j / 8) differs from i's by at most 5; the same strip row occurs only where the strip positions j mod 8 and i mod 8 differ by more than 2; entries may repeat. `parent_far`: entry of parent p names a parent q with |q - p| >= 6; entries may repeat.
All inputs are finite; a program needn't handle non-finite values.
Results may differ from the reference program's by a relative error of at most 0.0058.
Values may be sent and summed in bfloat16 or wider, within the bound.
A program may use at most 64 MiB of HBM per device.

```python
import jax
import jax.numpy as jnp
import numpy as np
from jax import lax

LEAF_SIZE = 256
RANK = 64
RIGHT_SIDES = 64
STRIP = 8
K_NEAR = 25
K_LEAF = 16
K_PARENT = 16
LEAVES_DEV = 128
LEAVES = 512
PARENTS = 64


offset_grid = np.array([[lateral - 2, vertical - 2] for vertical in range(5) for lateral in range(5) if vertical * 5 + lateral != 12], dtype=np.int32)


def near_lists(key):
    leaf_ids = jnp.arange(LEAVES, dtype=jnp.int32)
    lateral = leaf_ids % STRIP
    vertical = leaf_ids // STRIP
    strip_rows = LEAVES // STRIP
    shift_x = jnp.asarray(offset_grid[:, 0])[:, None]
    shift_y = jnp.asarray(offset_grid[:, 1])[:, None]
    target_x = lateral[None, :] + shift_x
    target_y = vertical[None, :] + shift_y
    inside = (target_x >= 0) & (target_x < STRIP) & (target_y >= 0) & (target_y < strip_rows)
    chosen = jax.random.randint(key, (24, LEAVES), 0, 4) > 0
    forced = (vertical == 2) & (lateral >= 2) & (lateral <= 5)
    keeping = inside & (chosen | forced[None, :])
    candidates = target_y * STRIP + target_x
    order_key = jnp.where(keeping, 0, 100) + jnp.arange(24, dtype=jnp.int32)[:, None]
    ordering = jnp.argsort(order_key, axis=0)
    kept_sorted = jnp.take_along_axis(keeping, ordering, axis=0)
    chosen_sorted = jnp.take_along_axis(candidates, ordering, axis=0)
    filled = jnp.where(kept_sorted, chosen_sorted, leaf_ids[None, :])
    listing = jnp.concatenate([leaf_ids[None, :], filled], axis=0).astype(jnp.int32)
    counts = (1 + jnp.sum(keeping.astype(jnp.int32), axis=0)).astype(jnp.int32)
    return (listing, counts)


def draw_near_list(key, part):
    return near_lists(key)[0]


def draw_near_count(key, part):
    return near_lists(key)[1]


def draw_points(key, part):
    key = jax.random.fold_in(key, 11)
    unit = jax.random.uniform(key, (3, LEAF_SIZE, LEAVES), jnp.float32, -1.0, 1.0)
    extent = jnp.array([24.0, 24.0, 2.0], jnp.float32)[:, None, None]
    return (unit * extent).astype(jnp.bfloat16)


def draw_leaf_far(key, part):
    key = jax.random.fold_in(key, 23)
    first_key, second_key = jax.random.split(key)
    leaf_ids = jnp.arange(LEAVES, dtype=jnp.int32)
    lateral = leaf_ids % STRIP
    vertical = leaf_ids // STRIP
    strip_rows = LEAVES // STRIP
    step_y = jax.random.randint(first_key, (K_LEAF, LEAVES), -5, 6)
    column = jax.random.randint(second_key, (K_LEAF, LEAVES), 0, STRIP)
    inside = (jnp.abs(column - lateral[None, :]) <= 2) & (jnp.abs(step_y) <= 2)
    step_y = jnp.where(inside, jnp.where(step_y >= 0, step_y + 3, step_y - 3), step_y)
    target_y = vertical[None, :] + step_y
    target_y = jnp.where((target_y < 0) | (target_y >= strip_rows), vertical[None, :] - step_y, target_y)
    listing = target_y * STRIP + column
    first_slot = jnp.arange(K_LEAF, dtype=jnp.int32)[:, None] == 0
    listing = jnp.where(first_slot & (leaf_ids[None, :] == 3 * STRIP), 0, listing)
    listing = jnp.where(first_slot & (leaf_ids[None, :] == LEAVES - 1 - 3 * STRIP), LEAVES - 1, listing)
    return listing.astype(jnp.int32)


def draw_parent_far(key, part):
    key = jax.random.fold_in(key, 37)
    parent_ids = jnp.arange(PARENTS, dtype=jnp.int32)
    drawn = jax.random.randint(key, (K_PARENT, PARENTS), 0, PARENTS - 11)
    listing = jnp.where(drawn >= parent_ids[None, :] - 5, drawn + 11, drawn)
    first_slot = jnp.arange(K_PARENT, dtype=jnp.int32)[:, None] == 0
    listing = jnp.where(first_slot & (parent_ids[None, :] == 6), 0, listing)
    listing = jnp.where(first_slot & (parent_ids[None, :] == PARENTS - 7), PARENTS - 1, listing)
    return listing.astype(jnp.int32)


def block_scale(key, shape, pieces, low, top_value):
    level = 1.0
    for axis_at, shards_of in pieces:
        draws = jax.random.uniform(jax.random.fold_in(jax.random.fold_in(key, 6), axis_at), (shards_of,), jnp.float32, low / len(pieces), top_value / len(pieces))
        level = level * jnp.repeat(jnp.exp(draws), shape[axis_at] // shards_of).reshape((-1,) + (1,) * (len(shape) - 1 - axis_at))
    return level


def gaussian(key, shape, deviation, reach, cuts=(), kind=jnp.bfloat16):
    result = deviation * jax.random.normal(key, shape, jnp.float32)
    if cuts:
        result = result * block_scale(key, shape, cuts, -0.22, 0.18)
    return jnp.clip(result, -reach, reach).astype(kind)


def setup_inputs(seed: int = 0, part: int = 0) -> dict:
    key_of = jax.random.split(jax.random.key(seed), 11)
    part_splits = jax.random.split(jax.random.fold_in(key_of[10], part), 11)
    return {
        "points": draw_points(jax.random.fold_in(jax.random.fold_in(key_of[10], part), 71), part),
        "charges": gaussian(part_splits[1], (LEAF_SIZE, RIGHT_SIDES, LEAVES), 1.0, 6.0, ((0, 2), (1, 2), (2, 4))),
        "basis": gaussian(part_splits[2], (LEAF_SIZE, RANK, LEAVES), LEAF_SIZE ** -0.5, 0.375, ((0, 2), (2, 4))),
        "transfer": gaussian(part_splits[3], (RANK, RANK, LEAVES), (RANK * STRIP) ** -0.5, 0.25, ((2, 4),)),
        "leaf_skeleton": jnp.clip(jax.random.uniform(part_splits[4], (3, RANK, LEAVES), jnp.float32, -2.0, 2.0) * block_scale(part_splits[4], (3, RANK, LEAVES), ((2, 4),), -0.4, 0.0), -2.0, 2.0).astype(jnp.bfloat16),
        "parent_skeleton": jnp.clip(jax.random.uniform(part_splits[5], (3, RANK, PARENTS), jnp.float32, -2.0, 2.0) * block_scale(part_splits[5], (3, RANK, PARENTS), ((2, 4),), -0.4, 0.0), -2.0, 2.0).astype(jnp.bfloat16),
        "near_list": draw_near_list(jax.random.fold_in(jax.random.fold_in(key_of[10], part), 71), part),
        "near_count": draw_near_count(jax.random.fold_in(jax.random.fold_in(key_of[10], part), 71), part),
        "leaf_far": draw_leaf_far(jax.random.fold_in(jax.random.fold_in(key_of[10], part), 71), part),
        "parent_far": draw_parent_far(jax.random.fold_in(jax.random.fold_in(key_of[10], part), 71), part),
    }


near_scale = 0.25
coupling_scale = 0.0625
softening = 0.25
spacing = 16.0

def element_kernel(row_points, row_ids, col_points, col_ids):
    shift_x = (row_ids % STRIP - col_ids % STRIP).astype(jnp.float32) * spacing
    shift_y = (row_ids // STRIP - col_ids // STRIP).astype(jnp.float32) * spacing
    shifts = (shift_x, shift_y, jnp.zeros_like(shift_x))
    running = jnp.zeros((row_points.shape[1], col_points.shape[1], row_ids.shape[0]), jnp.float32)
    for component in range(3):
        offset_gap = row_points[component].astype(jnp.float32)[:, None, :] - col_points[component].astype(jnp.float32)[None, :, :]
        offset_gap = offset_gap + shifts[component][None, None, :]
        running = running + offset_gap * offset_gap
    return near_scale / jnp.sqrt(running + softening)

def skeleton_kernel(targets, sources):
    running = jnp.zeros((targets.shape[1], sources.shape[1], targets.shape[2]), jnp.float32)
    for component in range(3):
        offset_gap = targets[component].astype(jnp.float32)[:, None, :] - sources[component].astype(jnp.float32)[None, :, :]
        running = running + offset_gap * offset_gap
    return coupling_scale / jnp.sqrt(running + softening)

def near_field(points, charges, near_list, near_count):
    leaf_ids = jnp.arange(LEAVES, dtype=jnp.int32)

    def one_block(block_index):
        start = block_index * LEAVES_DEV
        row_points = lax.dynamic_slice_in_dim(points, start, LEAVES_DEV, 2)
        row_ids = lax.dynamic_slice_in_dim(leaf_ids, start, LEAVES_DEV, 0)
        listing = lax.dynamic_slice_in_dim(near_list, start, LEAVES_DEV, 1)
        counts = lax.dynamic_slice_in_dim(near_count, start, LEAVES_DEV, 0)

        def near_step(running, position):
            source_ids = listing[position]
            near_tile = element_kernel(row_points, row_ids, jnp.take(points, source_ids, axis=2), source_ids)
            near_tile = jnp.where((position < counts)[None, None, :], near_tile, 0.0).astype(jnp.bfloat16)
            sources = jnp.take(charges, source_ids, axis=2)
            running = running + jnp.einsum('rsi,sci->rci', near_tile.astype(jnp.float32), sources.astype(jnp.float32))
            return (running, None)
        initial = jnp.zeros((LEAF_SIZE, RIGHT_SIDES, LEAVES_DEV), jnp.float32)
        running, _ = lax.scan(near_step, initial, jnp.arange(K_NEAR, dtype=jnp.int32))
        return running
    blocks = lax.map(one_block, jnp.arange(LEAVES // LEAVES_DEV, dtype=jnp.int32))
    return jnp.transpose(blocks, (1, 2, 0, 3)).reshape(LEAF_SIZE, RIGHT_SIDES, LEAVES)

def coupling_field(skeleton, moments, far_list):

    def far_step(running, position):
        source_ids = far_list[position]
        far_tile = skeleton_kernel(skeleton, jnp.take(skeleton, source_ids, axis=2)).astype(jnp.bfloat16)
        sources = jnp.take(moments, source_ids, axis=2)
        running = running + jnp.einsum('abi,bci->aci', far_tile.astype(jnp.float32), sources.astype(jnp.float32))
        return (running, None)
    initial = jnp.zeros((RANK, RIGHT_SIDES, far_list.shape[1]), jnp.float32)
    running, _ = lax.scan(far_step, initial, jnp.arange(far_list.shape[0], dtype=jnp.int32))
    return running

def reference(points, charges, basis, transfer, leaf_skeleton, parent_skeleton, near_list, near_count, leaf_far, parent_far):
    near_part = near_field(points, charges, near_list, near_count)
    moments0 = jnp.einsum('sai,sci->aci', basis.astype(jnp.float32), charges.astype(jnp.float32)).astype(jnp.bfloat16)
    lifted = jnp.einsum('abi,aci->bci', transfer.astype(jnp.float32), moments0.astype(jnp.float32))
    moments1 = lifted.reshape(RANK, RIGHT_SIDES, PARENTS, STRIP).sum(axis=3).astype(jnp.bfloat16)
    field0 = coupling_field(leaf_skeleton, moments0, leaf_far)
    field1 = coupling_field(parent_skeleton, moments1, parent_far)
    parent_field = field1.astype(jnp.bfloat16)
    spread = jnp.broadcast_to(parent_field[:, :, :, None], (RANK, RIGHT_SIDES, PARENTS, STRIP)).reshape(RANK, RIGHT_SIDES, LEAVES)
    leaf_field = (field0 + jnp.einsum('abi,bci->aci', transfer.astype(jnp.float32), spread.astype(jnp.float32))).astype(jnp.bfloat16)
    far_part = jnp.einsum('sai,aci->sci', basis.astype(jnp.float32), leaf_field.astype(jnp.float32))
    return (near_part + far_part).astype(jnp.bfloat16)
```

```python
import functools

import jax
import jax.numpy as jnp
import numpy as np
from jax import lax
from jax.experimental import pallas as pl
from jax.experimental.pallas import tpu as pltpu
from jax.sharding import PartitionSpec as P

STRIP = 8
GROUP = 4
FEATURES = 16

softening = 0.25
spacing = 16.0
near_power = 16.0
far_power = 256.0


def padded(cells, axis, width):
    count = lax.axis_size(axis)
    ends = count - 1
    head = cells[:width]
    tail = cells[cells.shape[0] - width :]
    return jnp.concatenate(
        [
            lax.ppermute(tail, axis, [(i, i + 1) for i in range(ends)]),
            cells,
            lax.ppermute(head, axis, [(i + 1, i) for i in range(ends)]),
        ],
        axis=0,
    )


def rotated(cells, axis, step):
    count = lax.axis_size(axis)
    return lax.ppermute(cells, axis, [((i + step) % count, i) for i in range(count)])


def paired(cells, axis_index, dim):
    other = rotated(cells, "rhs", 1)
    first = axis_index == 0
    return jnp.concatenate(
        [jnp.where(first, cells, other), jnp.where(first, other, cells)], axis=dim
    )


def pieces(value):
    top = value.astype(jnp.bfloat16).astype(jnp.float32)
    middle = (value - top).astype(jnp.bfloat16).astype(jnp.float32)
    return [top, middle, value - top - middle]


def offset_tables(width):
    factor = np.zeros((26, FEATURES), np.float32)
    added = np.zeros((26, FEATURES), np.float32)
    factor[:, :9] = 1.0
    factor[:, 14] = 1.0
    for o in range(25):
        shift_x = -spacing * (o % 5 - 2)
        shift_y = -spacing * (o // 5 - 2)
        factor[o, 11] = -2.0 * shift_x
        factor[o, 12] = -2.0 * shift_y
        added[o, 9] = 2.0 * shift_x * near_power
        added[o, 10] = 2.0 * shift_y * near_power
        added[o, 13] = (shift_x * shift_x + shift_y * shift_y) * near_power
    added[25, 13] = np.inf
    spread = lambda t: jnp.asarray(np.repeat(t[:, :, None], width, axis=2), jnp.bfloat16)
    return spread(factor), spread(added)


def row_features(cells):
    x, y, z = cells[0:1], cells[1:2], cells[2:3]
    one = jnp.ones_like(x)
    norm = pieces(x * x + y * y + z * z)
    parts = [x, y, z] + norm + [one] * 3 + [x, y] + [one] * 4 + [jnp.zeros_like(x)]
    return jnp.concatenate(parts, axis=0)


def column_features(cells, power, shifted):
    x, y, z = cells[0:1], cells[1:2], cells[2:3]
    one = jnp.ones_like(x)
    zero = jnp.zeros_like(x)
    norm = pieces(x * x + y * y + z * z)
    parts = (
        [-2.0 * x, -2.0 * y, -2.0 * z]
        + [one] * 3
        + norm
        + [zero, zero]
        + ([x, y] if shifted else [zero, zero])
        + [zero, softening * one, zero]
    )
    return jnp.concatenate(parts, axis=0) * power


def near_kernel(
    slots,
    shares,
    codes_ref,
    groups_ref,
    own_ref,
    border_ref,
    factor_ref,
    added_ref,
    *refs,
):
    charge_refs = refs[:shares]
    out_ref, base_ref, rows_ref, tiles_ref, leaf_at, code_at = refs[shares:]
    leaves = out_ref.shape[0]
    width = border_ref.shape[2]

    def base_step(j, _):
        base_ref[j] = column_features(border_ref[j], near_power, True).astype(jnp.bfloat16)
        return 0

    lax.fori_loop(0, border_ref.shape[0], base_step, 0, unroll=2)

    def row_step(i, at):
        rows_ref[i] = jnp.transpose(row_features(own_ref[i])).astype(jnp.bfloat16)
        out_ref[i] = jnp.zeros(out_ref.shape[1:], jnp.float32)

        def list_step(g, at):
            leaf_at[at] = i
            code_at[at] = i * slots + g * GROUP
            return at + 1

        return lax.fori_loop(0, groups_ref[i], list_step, at)

    total = lax.fori_loop(0, leaves, row_step, 0)
    for spare in range(3):
        leaf_at[total + spare] = 0
        code_at[total + spare] = leaves * slots

    def tile_stage(at, slot):
        row = rows_ref[leaf_at[at]]
        start = code_at[at]
        for u in range(GROUP):
            code = codes_ref[start + u]
            column = base_ref[code // 32] * factor_ref[code % 32] + added_ref[code % 32]
            square = jnp.dot(row, column, preferred_element_type=jnp.float32)
            tiles_ref[slot, :, u * width : (u + 1) * width] = lax.rsqrt(square).astype(jnp.bfloat16)

    def sum_stage(at, slot):
        start = code_at[at]
        i = leaf_at[at]
        sources = []
        for u in range(GROUP):
            j = codes_ref[start + u] // 32
            sources += [ref[j] for ref in charge_refs]
        out_ref[i] += lax.dot_general(
            tiles_ref[slot],
            jnp.concatenate(sources, axis=1),
            (((1,), (1,)), ((), ())),
            preferred_element_type=jnp.float32,
        )

    tile_stage(0, 0)

    def pair_step(t, _):
        at = 2 * t
        tile_stage(at + 1, 1)
        sum_stage(at, 0)
        tile_stage(at + 2, 0)
        sum_stage(at + 1, 1)
        return 0

    lax.fori_loop(0, (total + 1) // 2, pair_step, 0)


def far_kernel(
    leaf_slots,
    parent_slots,
    leaf_reach,
    leaf_ids_ref,
    parent_ids_ref,
    own_start_ref,
    leaf_skeleton_ref,
    leaf_moments_ref,
    parent_skeleton_ref,
    parent_moments_ref,
    transfer_ref,
    basis_ref,
    near_ref,
    out_ref,
    leaf_cols_ref,
    parent_cols_ref,
):
    parents = out_ref.shape[0] // STRIP

    def fill(skeleton_ref, cols_ref):
        def step(j, _):
            columns = column_features(skeleton_ref[j], far_power, False)
            cols_ref[j] = jnp.transpose(columns).astype(jnp.bfloat16)
            return 0

        lax.fori_loop(0, skeleton_ref.shape[0], step, 0, unroll=2)

    fill(leaf_skeleton_ref, leaf_cols_ref)
    fill(parent_skeleton_ref, parent_cols_ref)

    def coupled(cells, slots, start, ids_ref, cols_ref, moments_ref):
        row = jnp.transpose(row_features(cells)).astype(jnp.bfloat16)
        ids = [ids_ref[start + u] for u in range(slots)]
        column = jnp.concatenate([cols_ref[j] for j in ids], axis=0)
        square = lax.dot_general(
            row, column, (((1,), (1,)), ((), ())), preferred_element_type=jnp.float32
        )
        return jnp.dot(
            lax.rsqrt(square).astype(jnp.bfloat16),
            jnp.concatenate([moments_ref[j] for j in ids], axis=0),
            preferred_element_type=jnp.float32,
        )

    def parent_step(p, _):
        parent_field = coupled(
            parent_skeleton_ref[own_start_ref[0] + p],
            parent_slots,
            p * parent_slots,
            parent_ids_ref,
            parent_cols_ref,
            parent_moments_ref,
        ).astype(jnp.bfloat16)

        def leaf_step(child, _):
            i = p * STRIP + child
            field = coupled(
                leaf_skeleton_ref[leaf_reach + i],
                leaf_slots,
                i * leaf_slots,
                leaf_ids_ref,
                leaf_cols_ref,
                leaf_moments_ref,
            )
            leaf_field = field + jnp.dot(
                transfer_ref[i], parent_field, preferred_element_type=jnp.float32
            )
            far = jnp.dot(
                basis_ref[i], leaf_field.astype(jnp.bfloat16), preferred_element_type=jnp.float32
            )
            out_ref[i] = (near_ref[i] + far).astype(out_ref.dtype)
            return 0

        lax.fori_loop(0, STRIP, leaf_step, 0, unroll=4)
        return 0

    lax.fori_loop(0, parents, parent_step, 0)


def in_smem(count):
    return [pl.BlockSpec(memory_space=pltpu.SMEM)] * count


def in_vmem(count):
    return [pl.BlockSpec(memory_space=pltpu.VMEM)] * count


def per_device(
    points,
    charges,
    basis,
    transfer,
    leaf_skeleton,
    parent_skeleton,
    near_list,
    near_count,
    leaf_far,
    parent_far,
):
    rows_here, columns, leaf_count = charges.shape
    rank_size = basis.shape[1]
    near_index = lax.axis_index("near")
    leaf_index = lax.axis_index("leaf")
    rhs_index = lax.axis_index("rhs")
    rhs_parts = lax.axis_size("rhs")
    near_reach = 2 * STRIP + 2
    far_reach = 6 * STRIP - 1
    own = leaf_count // rhs_parts
    own_parents = own // STRIP
    own_start = rhs_index * own
    first_leaf = leaf_index * leaf_count + own_start
    all_columns = columns * rhs_parts

    def mine(array, dim, width=own, start=own_start):
        return lax.dynamic_slice_in_dim(array, start, width, dim)

    leaf_parts = lax.axis_size("leaf")
    near_parts = lax.axis_size("near")
    window = own + 2 * near_reach

    wide = paired(jnp.transpose(charges, (2, 1, 0)), rhs_index, 1)
    wide = mine(padded(wide, "leaf", near_reach), 0, window)
    shares = [wide] + [rotated(wide, "near", k) for k in range(1, near_parts)]

    point_cells = jnp.transpose(points, (2, 0, 1))
    border_points = mine(padded(point_cells, "leaf", near_reach), 0, window)
    twice = jnp.concatenate([border_points, border_points], axis=2).astype(jnp.float32)
    border_points = mine(twice, 2, point_cells.shape[2], near_index * rows_here)
    own_points = border_points[near_reach : near_reach + own, :, :rows_here]

    listing = mine(near_list, 1)
    counts = mine(near_count, 0)
    row_ids = first_leaf + jnp.arange(own, dtype=jnp.int32)
    live = jnp.arange(near_list.shape[0], dtype=jnp.int32)[:, None] < counts[None, :]
    offset = (
        (listing % STRIP - row_ids[None, :] % STRIP + 2)
        + 5 * (listing // STRIP - row_ids[None, :] // STRIP + 2)
    )
    code = jnp.where(live, (listing - (first_leaf - near_reach)) * 32 + offset, 25)
    slots = -(-near_list.shape[0] // GROUP) * GROUP
    code = jnp.pad(
        jnp.transpose(code), ((0, 1), (0, slots - near_list.shape[0])), constant_values=25
    ).reshape(-1)
    groups = (counts + (GROUP - 1)) // GROUP
    factor, added = offset_tables(border_points.shape[2])

    basis_cells = jnp.transpose(mine(basis, 2), (2, 0, 1))
    own_charges = lax.slice_in_dim(wide, near_reach, near_reach + own, axis=0)
    partial = jnp.einsum(
        "isa,ics->iac", basis_cells, own_charges, preferred_element_type=jnp.float32
    )
    sent = partial.astype(jnp.bfloat16)
    for k in range(1, near_parts):
        partial = partial + rotated(sent, "near", k).astype(jnp.float32)
    moments0 = partial.astype(jnp.bfloat16)
    transfer_cells = jnp.transpose(mine(transfer, 2), (2, 0, 1))
    moments1 = jnp.einsum(
        "pkb,pkc->pbc",
        transfer_cells.reshape(own_parents, STRIP * rank_size, rank_size),
        moments0.reshape(own_parents, STRIP * rank_size, all_columns),
        preferred_element_type=jnp.float32,
    ).astype(jnp.bfloat16)
    chip_parents = paired(moments1, rhs_index, 0)
    turn = lambda cells: jnp.concatenate(
        [cells] + [rotated(cells, "leaf", k) for k in range(1, leaf_parts)], axis=0
    )
    every_moments = turn(chip_parents)
    chip_moments = paired(moments0, rhs_index, 0)
    border_moments = mine(padded(chip_moments, "leaf", far_reach), 0, own + 2 * far_reach)

    near_part = pl.pallas_call(
        functools.partial(near_kernel, slots, near_parts),
        out_shape=jax.ShapeDtypeStruct((own, rows_here, all_columns), jnp.float32),
        in_specs=in_smem(2) + in_vmem(4 + near_parts),
        out_specs=pl.BlockSpec(memory_space=pltpu.VMEM),
        scratch_shapes=[
            pltpu.VMEM((window, FEATURES, border_points.shape[2]), jnp.bfloat16),
            pltpu.VMEM((own, rows_here, FEATURES), jnp.bfloat16),
            pltpu.VMEM((2, rows_here, GROUP * border_points.shape[2]), jnp.bfloat16),
            pltpu.SMEM((own * (slots // GROUP) + 3,), jnp.int32),
            pltpu.SMEM((own * (slots // GROUP) + 3,), jnp.int32),
        ],
        compiler_params=pltpu.CompilerParams(vmem_limit_bytes=48 * 2**20),
        cost_estimate=pl.CostEstimate(
            flops=60 * 10**9, bytes_accessed=16 * 10**6, transcendentals=0
        ),
        name="near_field",
    )(code, groups, own_points, border_points, factor, added, *shares)

    skeleton_cells = jnp.transpose(leaf_skeleton, (2, 0, 1))
    border_skeleton = mine(padded(skeleton_cells, "leaf", far_reach), 0, own + 2 * far_reach)
    parent_cells = jnp.transpose(parent_skeleton, (2, 0, 1))
    every_skeleton = turn(parent_cells)
    parent_start = rhs_index * own_parents
    leaf_ids = jnp.transpose(mine(leaf_far, 1) - (first_leaf - far_reach)).reshape(-1)
    chip_count = parent_far.shape[1]
    parent_ids = jnp.transpose(mine(parent_far, 1, own_parents, parent_start)).reshape(-1)
    parent_ids = (parent_ids + (leaf_parts - leaf_index) * chip_count) % (leaf_parts * chip_count)

    result = pl.pallas_call(
        functools.partial(far_kernel, leaf_far.shape[0], parent_far.shape[0], far_reach),
        out_shape=jax.ShapeDtypeStruct((own, rows_here, all_columns), jnp.bfloat16),
        in_specs=in_smem(3) + in_vmem(7),
        out_specs=pl.BlockSpec(memory_space=pltpu.VMEM),
        scratch_shapes=[
            pltpu.VMEM((own + 2 * far_reach, rank_size, FEATURES), jnp.bfloat16),
            pltpu.VMEM((leaf_parts * chip_count, rank_size, FEATURES), jnp.bfloat16),
        ],
        compiler_params=pltpu.CompilerParams(vmem_limit_bytes=48 * 2**20),
        name="far_field",
    )(
        leaf_ids,
        parent_ids,
        parent_start.astype(jnp.int32).reshape(1),
        border_skeleton.astype(jnp.float32),
        border_moments,
        every_skeleton.astype(jnp.float32),
        every_moments,
        transfer_cells,
        basis_cells,
        near_part,
    )
    result = jnp.transpose(result, (1, 2, 0))
    kept = mine(result, 1, columns, rhs_index * columns)
    given = mine(result, 1, columns, (1 - rhs_index) * columns)
    taken = rotated(given, "rhs", 1)
    first = rhs_index == 0
    return jnp.concatenate(
        [jnp.where(first, kept, taken), jnp.where(first, taken, kept)], axis=2
    )


def solution(mesh):
    placed = (
        P(None, None, ("groups", "leaf")),
        P("near", "rhs", ("groups", "leaf")),
        P("near", None, ("groups", "leaf")),
        P(None, None, ("groups", "leaf")),
        P(None, None, ("groups", "leaf")),
        P(None, None, ("groups", "leaf")),
        P(None, ("groups", "leaf")),
        P(("groups", "leaf")),
        P(None, ("groups", "leaf")),
        P(None, ("groups", "leaf")),
    )
    return jax.shard_map(
        per_device,
        mesh=mesh,
        in_specs=placed,
        out_specs=P("near", "rhs", ("groups", "leaf")),
        check_vma=False,
    )
```

```python
import functools

import jax
import jax.numpy as jnp
import numpy as np
from jax import lax
from jax.experimental import pallas as pl
from jax.experimental.pallas import tpu as pltpu
from jax.sharding import PartitionSpec as P

STRIP = 8
GROUP = 4
FEATURES = 16
NEAR_CALLS = 2

softening = 0.25
spacing = 16.0
near_power = 16.0
far_power = 256.0


def halo(cells, axis, width):
    ends = lax.axis_size(axis) - 1
    head = cells[:width]
    tail = cells[cells.shape[0] - width :]
    return [
        lax.ppermute(tail, axis, [(i, i + 1) for i in range(ends)]),
        cells,
        lax.ppermute(head, axis, [(i + 1, i) for i in range(ends)]),
    ]


def padded(cells, axis, width):
    return jnp.concatenate(halo(cells, axis, width), axis=0)


def rotated(cells, axis, step):
    count = lax.axis_size(axis)
    return lax.ppermute(cells, axis, [((i + step) % count, i) for i in range(count)])


def paired(cells, axis_index, dim):
    other = rotated(cells, "rhs", 1)
    first = axis_index == 0
    return jnp.concatenate(
        [jnp.where(first, cells, other), jnp.where(first, other, cells)], axis=dim
    )


def pieces(value):
    top = value.astype(jnp.bfloat16).astype(jnp.float32)
    middle = (value - top).astype(jnp.bfloat16).astype(jnp.float32)
    return [top, middle, value - top - middle]


def offset_tables(width):
    factor = np.zeros((26, FEATURES), np.float32)
    added = np.zeros((26, FEATURES), np.float32)
    factor[:, :9] = 1.0
    factor[:, 14] = 1.0
    for o in range(25):
        shift_x = -spacing * (o % 5 - 2)
        shift_y = -spacing * (o // 5 - 2)
        factor[o, 11] = -2.0 * shift_x
        factor[o, 12] = -2.0 * shift_y
        added[o, 9] = 2.0 * shift_x * near_power
        added[o, 10] = 2.0 * shift_y * near_power
        added[o, 13] = (shift_x * shift_x + shift_y * shift_y) * near_power
    added[25, 13] = np.inf
    spread = lambda t: jnp.asarray(np.repeat(t[:, :, None], width, axis=2), jnp.bfloat16)
    return spread(factor), spread(added)


def row_features(cells):
    x, y, z = cells[0:1], cells[1:2], cells[2:3]
    one = jnp.ones_like(x)
    norm = pieces(x * x + y * y + z * z)
    parts = [x, y, z] + norm + [one] * 3 + [x, y] + [one] * 4 + [jnp.zeros_like(x)]
    return jnp.concatenate(parts, axis=0)


def column_features(cells, power, shifted):
    x, y, z = cells[0:1], cells[1:2], cells[2:3]
    one = jnp.ones_like(x)
    zero = jnp.zeros_like(x)
    norm = pieces(x * x + y * y + z * z)
    parts = (
        [-2.0 * x, -2.0 * y, -2.0 * z]
        + [one] * 3
        + norm
        + [zero, zero]
        + ([x, y] if shifted else [zero, zero])
        + [zero, softening * one, zero]
    )
    return jnp.concatenate(parts, axis=0) * power


def near_kernel(
    slots,
    shares,
    first_border,
    border_count,
    codes_ref,
    groups_ref,
    own_ref,
    border_ref,
    factor_ref,
    added_ref,
    *refs,
):
    charge_refs = refs[:shares]
    out_ref, base_ref, rows_ref, tiles_ref, leaf_at, code_at = refs[shares:]
    leaves = out_ref.shape[0]
    width = border_ref.shape[2]

    def base_step(j, _):
        base_ref[j] = column_features(border_ref[j], near_power, True).astype(jnp.bfloat16)
        return 0

    lax.fori_loop(first_border, first_border + border_count, base_step, 0, unroll=2)

    def row_step(i, at):
        rows_ref[i] = jnp.transpose(row_features(own_ref[i])).astype(jnp.bfloat16)
        out_ref[i] = jnp.zeros(out_ref.shape[1:], jnp.float32)

        def list_step(g, at):
            leaf_at[at] = i
            code_at[at] = i * slots + g * GROUP
            return at + 1

        return lax.fori_loop(0, groups_ref[i], list_step, at)

    total = lax.fori_loop(0, leaves, row_step, 0)
    for spare in range(3):
        leaf_at[total + spare] = 0
        code_at[total + spare] = leaves * slots

    def tile_stage(at, slot):
        row = rows_ref[leaf_at[at]]
        start = code_at[at]
        for u in range(GROUP):
            code = codes_ref[start + u]
            column = base_ref[code // 32] * factor_ref[code % 32] + added_ref[code % 32]
            square = jnp.dot(row, column, preferred_element_type=jnp.float32)
            tiles_ref[slot, :, u * width : (u + 1) * width] = lax.rsqrt(square.astype(jnp.bfloat16))

    def sum_stage(at, slot):
        start = code_at[at]
        i = leaf_at[at]
        sources = []
        for u in range(GROUP):
            j = codes_ref[start + u] // 32
            sources += [ref[j] for ref in charge_refs]
        out_ref[i] += lax.dot_general(
            tiles_ref[slot],
            jnp.concatenate(sources, axis=1),
            (((1,), (1,)), ((), ())),
            preferred_element_type=jnp.float32,
        )

    tile_stage(0, 0)

    def pair_step(t, _):
        at = 2 * t
        tile_stage(at + 1, 1)
        sum_stage(at, 0)
        tile_stage(at + 2, 0)
        sum_stage(at + 1, 1)
        return 0

    lax.fori_loop(0, (total + 1) // 2, pair_step, 0)


def far_kernel(
    leaf_slots,
    parent_slots,
    leaf_reach,
    leaf_ids_ref,
    parent_ids_ref,
    own_start_ref,
    leaf_skeleton_ref,
    leaf_moments_ref,
    parent_skeleton_ref,
    parent_moments_ref,
    transfer_ref,
    basis_ref,
    *refs,
):
    near_refs = refs[:NEAR_CALLS]
    out_ref, leaf_cols_ref, parent_cols_ref, rows_ref, tiles_ref, parent_field_ref, field_ref = refs[
        NEAR_CALLS:
    ]
    leaves = out_ref.shape[0]
    parents = leaves // STRIP

    def fill(skeleton_ref, cols_ref):
        def step(j, _):
            columns = column_features(skeleton_ref[j], far_power, False)
            cols_ref[j] = jnp.transpose(columns).astype(jnp.bfloat16)
            return 0

        lax.fori_loop(0, skeleton_ref.shape[0], step, 0, unroll=4)

    fill(leaf_skeleton_ref, leaf_cols_ref)
    fill(parent_skeleton_ref, parent_cols_ref)

    def row_step(i, _):
        rows_ref[i] = jnp.transpose(row_features(leaf_skeleton_ref[leaf_reach + i])).astype(
            jnp.bfloat16
        )
        return 0

    lax.fori_loop(0, leaves, row_step, 0, unroll=4)

    def stacked(slots, start, ids_ref, ref):
        return jnp.concatenate([ref[ids_ref[start + u]] for u in range(slots)], axis=0)

    def tile_of(row, column):
        square = lax.dot_general(
            row, column, (((1,), (1,)), ((), ())), preferred_element_type=jnp.float32
        )
        return lax.rsqrt(square).astype(jnp.bfloat16)

    def parent_step(p, _):
        start = p * parent_slots
        row = jnp.transpose(row_features(parent_skeleton_ref[own_start_ref[0] + p]))
        parent_field_ref[p] = jnp.dot(
            tile_of(
                row.astype(jnp.bfloat16),
                stacked(parent_slots, start, parent_ids_ref, parent_cols_ref),
            ),
            stacked(parent_slots, start, parent_ids_ref, parent_moments_ref),
            preferred_element_type=jnp.float32,
        ).astype(jnp.bfloat16)
        return 0

    lax.fori_loop(0, parents, parent_step, 0)

    def tile_stage(i, slot):
        tiles_ref[slot] = tile_of(
            rows_ref[i], stacked(leaf_slots, i * leaf_slots, leaf_ids_ref, leaf_cols_ref)
        )

    def sum_stage(i, slot):
        field = jnp.dot(
            tiles_ref[slot],
            stacked(leaf_slots, i * leaf_slots, leaf_ids_ref, leaf_moments_ref),
            preferred_element_type=jnp.float32,
        )
        spread = jnp.dot(
            transfer_ref[i], parent_field_ref[i // STRIP], preferred_element_type=jnp.float32
        )
        field_ref[i] = (field + spread).astype(jnp.bfloat16)

    tile_stage(0, 0)

    def pair_step(t, _):
        tile_stage(2 * t + 1, 1)
        sum_stage(2 * t, 0)
        tile_stage(jnp.minimum(2 * t + 2, leaves - 1), 0)
        sum_stage(2 * t + 1, 1)
        return 0

    lax.fori_loop(0, leaves // 2, pair_step, 0)

    share = leaves // NEAR_CALLS
    for part, near_ref in enumerate(near_refs):

        def last_step(k, _):
            i = part * share + k
            far = jnp.dot(basis_ref[i], field_ref[i], preferred_element_type=jnp.float32)
            out_ref[i] = jnp.transpose(near_ref[k] + far).astype(out_ref.dtype)
            return 0

        lax.fori_loop(0, share, last_step, 0, unroll=4)


def in_smem(count):
    return [pl.BlockSpec(memory_space=pltpu.SMEM)] * count


def in_vmem(count):
    return [pl.BlockSpec(memory_space=pltpu.VMEM)] * count


def per_device(
    points,
    charges,
    basis,
    transfer,
    leaf_skeleton,
    parent_skeleton,
    near_list,
    near_count,
    leaf_far,
    parent_far,
):
    rows_here, columns, leaf_count = charges.shape
    rank_size = basis.shape[1]
    near_index = lax.axis_index("near")
    leaf_index = lax.axis_index("leaf")
    rhs_index = lax.axis_index("rhs")
    rhs_parts = lax.axis_size("rhs")
    near_reach = 2 * STRIP + 2
    far_reach = 6 * STRIP - 1
    own = leaf_count // rhs_parts
    own_parents = own // STRIP
    own_start = rhs_index * own
    first_leaf = leaf_index * leaf_count + own_start
    all_columns = columns * rhs_parts

    def mine(array, dim, width=own, start=own_start):
        return lax.dynamic_slice_in_dim(array, start, width, dim)

    leaf_parts = lax.axis_size("leaf")
    near_parts = lax.axis_size("near")
    window = own + 2 * near_reach

    wide = paired(jnp.transpose(charges, (2, 1, 0)), rhs_index, 1)
    wide = mine(padded(wide, "leaf", near_reach), 0, window)
    shares = [wide] + [rotated(wide, "near", k) for k in range(1, near_parts)]

    point_cells = jnp.transpose(points, (2, 0, 1))
    border_points = mine(padded(point_cells, "leaf", near_reach), 0, window)
    twice = jnp.concatenate([border_points, border_points], axis=2).astype(jnp.float32)
    border_points = mine(twice, 2, point_cells.shape[2], near_index * rows_here)
    own_points = border_points[near_reach : near_reach + own, :, :rows_here]

    listing = mine(near_list, 1)
    counts = mine(near_count, 0)
    row_ids = first_leaf + jnp.arange(own, dtype=jnp.int32)
    live = jnp.arange(near_list.shape[0], dtype=jnp.int32)[:, None] < counts[None, :]
    offset = (
        (listing % STRIP - row_ids[None, :] % STRIP + 2)
        + 5 * (listing // STRIP - row_ids[None, :] // STRIP + 2)
    )
    share = own // NEAR_CALLS
    idle = jnp.arange(own, dtype=jnp.int32) // share * share * 32 + 25
    code = jnp.where(live, (listing - (first_leaf - near_reach)) * 32 + offset, idle[None, :])
    slots = -(-near_list.shape[0] // GROUP) * GROUP
    spare = jnp.broadcast_to(idle[:, None], (own, slots - near_list.shape[0]))
    code = jnp.concatenate([jnp.transpose(code), spare], axis=1).reshape(-1)
    groups = (counts + (GROUP - 1)) // GROUP
    factor, added = offset_tables(border_points.shape[2])

    def near_call(part, after):
        share = own // NEAR_CALLS
        first = part * share
        cut = lambda array, start, width: lax.slice_in_dim(array, start, start + width, axis=0)
        part_codes = jnp.concatenate(
            [
                cut(code, first * slots, share * slots),
                jnp.full((slots,), first * 32 + 25, jnp.int32),
            ]
        )
        part_groups, after = lax.optimization_barrier((cut(groups, first, share), after))
        field = pl.pallas_call(
            functools.partial(near_kernel, slots, near_parts, first, share + 2 * near_reach),
            out_shape=jax.ShapeDtypeStruct((share, rows_here, all_columns), jnp.float32),
            in_specs=in_smem(2) + in_vmem(4 + near_parts),
            out_specs=pl.BlockSpec(memory_space=pltpu.VMEM),
            scratch_shapes=[
                pltpu.VMEM((window, FEATURES, border_points.shape[2]), jnp.bfloat16),
                pltpu.VMEM((share, rows_here, FEATURES), jnp.bfloat16),
                pltpu.VMEM((2, rows_here, GROUP * border_points.shape[2]), jnp.bfloat16),
                pltpu.SMEM((share * (slots // GROUP) + 3,), jnp.int32),
                pltpu.SMEM((share * (slots // GROUP) + 3,), jnp.int32),
            ],
            compiler_params=pltpu.CompilerParams(vmem_limit_bytes=48 * 2**20),
            cost_estimate=pl.CostEstimate(
                flops=30 * 10**9, bytes_accessed=16 * 10**6, transcendentals=0
            ),
            name="near_field",
        )(part_codes, part_groups, cut(own_points, first, share), border_points, factor, added, *shares)
        return field, after

    basis_cells = jnp.transpose(mine(basis, 2), (2, 0, 1))
    own_charges = lax.slice_in_dim(wide, near_reach, near_reach + own, axis=0)
    partial = jnp.einsum(
        "isa,ics->iac", basis_cells, own_charges, preferred_element_type=jnp.float32
    )
    sent = partial.astype(jnp.bfloat16)
    arrived = [rotated(sent, "near", k) for k in range(1, near_parts)]
    near_first, partial = near_call(0, partial)
    near_first, arrived = lax.optimization_barrier((near_first, arrived))
    for other in arrived:
        partial = partial + other.astype(jnp.float32)
    moments0 = partial.astype(jnp.bfloat16)
    transfer_cells = jnp.transpose(mine(transfer, 2), (2, 0, 1))
    moments1 = jnp.einsum(
        "pkb,pkc->pbc",
        transfer_cells.reshape(own_parents, STRIP * rank_size, rank_size),
        moments0.reshape(own_parents, STRIP * rank_size, all_columns),
        preferred_element_type=jnp.float32,
    ).astype(jnp.bfloat16)
    chip_parents = paired(moments1, rhs_index, 0)
    turned = lambda cells: [cells] + [rotated(cells, "leaf", k) for k in range(1, leaf_parts)]
    every_moments = turned(chip_parents)
    chip_moments = paired(moments0, rhs_index, 0)
    border_moments = halo(chip_moments, "leaf", far_reach)
    near_second, chip_moments = near_call(1, chip_moments)
    near_second, every_moments, border_moments = lax.optimization_barrier(
        (near_second, every_moments, border_moments)
    )
    every_moments = jnp.concatenate(every_moments, axis=0)
    border_moments = mine(jnp.concatenate(border_moments, axis=0), 0, own + 2 * far_reach)

    skeleton_cells = jnp.transpose(leaf_skeleton, (2, 0, 1))
    border_skeleton = mine(padded(skeleton_cells, "leaf", far_reach), 0, own + 2 * far_reach)
    parent_cells = jnp.transpose(parent_skeleton, (2, 0, 1))
    every_skeleton = jnp.concatenate(turned(parent_cells), axis=0)
    parent_start = rhs_index * own_parents
    leaf_ids = jnp.transpose(mine(leaf_far, 1) - (first_leaf - far_reach)).reshape(-1)
    chip_count = parent_far.shape[1]
    parent_ids = jnp.transpose(mine(parent_far, 1, own_parents, parent_start)).reshape(-1)
    parent_ids = (parent_ids + (leaf_parts - leaf_index) * chip_count) % (leaf_parts * chip_count)

    result = pl.pallas_call(
        functools.partial(far_kernel, leaf_far.shape[0], parent_far.shape[0], far_reach),
        out_shape=jax.ShapeDtypeStruct((own, all_columns, rows_here), jnp.bfloat16),
        in_specs=in_smem(3) + in_vmem(6 + NEAR_CALLS),
        out_specs=pl.BlockSpec(memory_space=pltpu.VMEM),
        scratch_shapes=[
            pltpu.VMEM((own + 2 * far_reach, rank_size, FEATURES), jnp.bfloat16),
            pltpu.VMEM((leaf_parts * chip_count, rank_size, FEATURES), jnp.bfloat16),
            pltpu.VMEM((own, rank_size, FEATURES), jnp.bfloat16),
            pltpu.VMEM((2, rank_size, leaf_far.shape[0] * rank_size), jnp.bfloat16),
            pltpu.VMEM((own_parents, rank_size, all_columns), jnp.bfloat16),
            pltpu.VMEM((own, rank_size, all_columns), jnp.bfloat16),
        ],
        compiler_params=pltpu.CompilerParams(vmem_limit_bytes=48 * 2**20),
        name="far_field",
    )(
        leaf_ids,
        parent_ids,
        parent_start.astype(jnp.int32).reshape(1),
        border_skeleton.astype(jnp.float32),
        border_moments,
        every_skeleton.astype(jnp.float32),
        every_moments,
        transfer_cells,
        basis_cells,
        near_first,
        near_second,
    )
    kept = mine(result, 1, columns, rhs_index * columns)
    given = mine(result, 1, columns, (1 - rhs_index) * columns)
    taken = rotated(given, "rhs", 1)
    first = rhs_index == 0
    result = jnp.concatenate(
        [jnp.where(first, kept, taken), jnp.where(first, taken, kept)], axis=0
    )
    return jnp.transpose(result, (2, 1, 0))


def solution(mesh):
    placed = (
        P(None, None, ("groups", "leaf")),
        P("near", "rhs", ("groups", "leaf")),
        P("near", None, ("groups", "leaf")),
        P(None, None, ("groups", "leaf")),
        P(None, None, ("groups", "leaf")),
        P(None, None, ("groups", "leaf")),
        P(None, ("groups", "leaf")),
        P(("groups", "leaf")),
        P(None, ("groups", "leaf")),
        P(None, ("groups", "leaf")),
    )
    return jax.shard_map(
        per_device,
        mesh=mesh,
        in_specs=placed,
        out_specs=P("near", "rhs", ("groups", "leaf")),
        check_vma=False,
    )
```

```python
import functools

import jax
import jax.numpy as jnp
import numpy as np
from jax import lax
from jax.experimental import pallas as pl
from jax.experimental.pallas import tpu as pltpu
from jax.sharding import PartitionSpec as P

STRIP = 8
GROUP = 4
FEATURES = 16
NEAR_CALLS = 2

softening = 0.25
spacing = 16.0
near_power = 16.0
far_power = 256.0


def halo(cells, axis, width):
    ends = lax.axis_size(axis) - 1
    head = cells[:width]
    tail = cells[cells.shape[0] - width :]
    return [
        lax.ppermute(tail, axis, [(i, i + 1) for i in range(ends)]),
        cells,
        lax.ppermute(head, axis, [(i + 1, i) for i in range(ends)]),
    ]


def padded(cells, axis, width):
    return jnp.concatenate(halo(cells, axis, width), axis=0)


def rotated(cells, axis, step):
    count = lax.axis_size(axis)
    return lax.ppermute(cells, axis, [((i + step) % count, i) for i in range(count)])


def paired(cells, axis_index, dim):
    other = rotated(cells, "rhs", 1)
    first = axis_index == 0
    return jnp.concatenate(
        [jnp.where(first, cells, other), jnp.where(first, other, cells)], axis=dim
    )


def pieces(value):
    top = value.astype(jnp.bfloat16).astype(jnp.float32)
    middle = (value - top).astype(jnp.bfloat16).astype(jnp.float32)
    return [top, middle, value - top - middle]


def offset_tables(width):
    factor = np.zeros((26, FEATURES), np.float32)
    added = np.zeros((26, FEATURES), np.float32)
    factor[:, :9] = 1.0
    factor[:, 14] = 1.0
    for o in range(25):
        shift_x = -spacing * (o % 5 - 2)
        shift_y = -spacing * (o // 5 - 2)
        factor[o, 11] = -2.0 * shift_x
        factor[o, 12] = -2.0 * shift_y
        added[o, 9] = 2.0 * shift_x * near_power
        added[o, 10] = 2.0 * shift_y * near_power
        added[o, 13] = (shift_x * shift_x + shift_y * shift_y) * near_power
    added[25, 13] = np.inf
    spread = lambda t: jnp.asarray(np.repeat(t[:, :, None], width, axis=2), jnp.bfloat16)
    return spread(factor), spread(added)


def row_features(cells):
    x, y, z = cells[0:1], cells[1:2], cells[2:3]
    one = jnp.ones_like(x)
    norm = pieces(x * x + y * y + z * z)
    parts = [x, y, z] + norm + [one] * 3 + [x, y] + [one] * 4 + [jnp.zeros_like(x)]
    return jnp.concatenate(parts, axis=0)


def column_features(cells, power, shifted):
    x, y, z = cells[0:1], cells[1:2], cells[2:3]
    one = jnp.ones_like(x)
    zero = jnp.zeros_like(x)
    norm = pieces(x * x + y * y + z * z)
    parts = (
        [-2.0 * x, -2.0 * y, -2.0 * z]
        + [one] * 3
        + norm
        + [zero, zero]
        + ([x, y] if shifted else [zero, zero])
        + [zero, softening * one, zero]
    )
    return jnp.concatenate(parts, axis=0) * power


def near_kernel(
    slots,
    shares,
    first_border,
    border_count,
    codes_ref,
    groups_ref,
    own_ref,
    border_ref,
    factor_ref,
    added_ref,
    *refs,
):
    charge_refs = refs[:shares]
    out_ref, base_ref, rows_ref, tiles_ref, leaf_at, code_at = refs[shares:]
    leaves = out_ref.shape[0]
    width = border_ref.shape[2]

    def base_step(j, _):
        base_ref[j] = column_features(border_ref[j], near_power, True).astype(jnp.bfloat16)
        return 0

    lax.fori_loop(first_border, first_border + border_count, base_step, 0, unroll=2)

    def row_step(i, at):
        rows_ref[i] = jnp.transpose(row_features(own_ref[i])).astype(jnp.bfloat16)
        out_ref[i] = jnp.zeros(out_ref.shape[1:], jnp.float32)

        def list_step(g, at):
            leaf_at[at] = i
            code_at[at] = i * slots + g * GROUP
            return at + 1

        return lax.fori_loop(0, groups_ref[i], list_step, at)

    total = lax.fori_loop(0, leaves, row_step, 0)
    for spare in range(3):
        leaf_at[total + spare] = 0
        code_at[total + spare] = leaves * slots

    def tile_stage(at, slot):
        row = rows_ref[leaf_at[at]]
        start = code_at[at]
        for u in range(GROUP):
            code = codes_ref[start + u]
            column = base_ref[code // 32] * factor_ref[code % 32] + added_ref[code % 32]
            square = jnp.dot(row, column, preferred_element_type=jnp.float32)
            tiles_ref[slot, :, u * width : (u + 1) * width] = lax.rsqrt(square.astype(jnp.bfloat16))

    def sum_stage(at, slot):
        start = code_at[at]
        i = leaf_at[at]
        sources = []
        for u in range(GROUP):
            j = codes_ref[start + u] // 32
            sources += [ref[j] for ref in charge_refs]
        out_ref[i] += lax.dot_general(
            tiles_ref[slot],
            jnp.concatenate(sources, axis=1),
            (((1,), (1,)), ((), ())),
            preferred_element_type=jnp.float32,
        )

    tile_stage(0, 0)

    def pair_step(t, _):
        at = 2 * t
        tile_stage(at + 1, 1)
        sum_stage(at, 0)
        tile_stage(at + 2, 0)
        sum_stage(at + 1, 1)
        return 0

    lax.fori_loop(0, (total + 1) // 2, pair_step, 0)


def far_kernel(
    leaf_slots,
    parent_slots,
    leaf_reach,
    leaf_ids_ref,
    parent_ids_ref,
    own_start_ref,
    leaf_skeleton_ref,
    leaf_moments_ref,
    parent_skeleton_ref,
    parent_moments_ref,
    transfer_ref,
    basis_ref,
    *refs,
):
    near_refs = refs[:NEAR_CALLS]
    out_ref, leaf_cols_ref, parent_cols_ref, rows_ref, tiles_ref, parent_field_ref, field_ref = refs[
        NEAR_CALLS:
    ]
    leaves = out_ref.shape[0]
    parents = leaves // STRIP

    def fill(skeleton_ref, cols_ref):
        def step(j, _):
            columns = column_features(skeleton_ref[j], far_power, False)
            cols_ref[j] = jnp.transpose(columns).astype(jnp.bfloat16)
            return 0

        lax.fori_loop(0, skeleton_ref.shape[0], step, 0, unroll=4)

    fill(leaf_skeleton_ref, leaf_cols_ref)
    fill(parent_skeleton_ref, parent_cols_ref)

    def row_step(i, _):
        rows_ref[i] = jnp.transpose(row_features(leaf_skeleton_ref[leaf_reach + i])).astype(
            jnp.bfloat16
        )
        return 0

    lax.fori_loop(0, leaves, row_step, 0, unroll=4)

    def stacked(slots, start, ids_ref, ref):
        return jnp.concatenate([ref[ids_ref[start + u]] for u in range(slots)], axis=0)

    def tile_of(row, column):
        square = lax.dot_general(
            row, column, (((1,), (1,)), ((), ())), preferred_element_type=jnp.float32
        )
        return lax.rsqrt(square).astype(jnp.bfloat16)

    def parent_step(p, _):
        start = p * parent_slots
        row = jnp.transpose(row_features(parent_skeleton_ref[own_start_ref[0] + p]))
        parent_field_ref[p] = jnp.dot(
            tile_of(
                row.astype(jnp.bfloat16),
                stacked(parent_slots, start, parent_ids_ref, parent_cols_ref),
            ),
            stacked(parent_slots, start, parent_ids_ref, parent_moments_ref),
            preferred_element_type=jnp.float32,
        ).astype(jnp.bfloat16)
        return 0

    lax.fori_loop(0, parents, parent_step, 0)

    def tile_stage(i, slot):
        tiles_ref[slot] = tile_of(
            rows_ref[i], stacked(leaf_slots, i * leaf_slots, leaf_ids_ref, leaf_cols_ref)
        )

    def sum_stage(i, slot):
        field = jnp.dot(
            tiles_ref[slot],
            stacked(leaf_slots, i * leaf_slots, leaf_ids_ref, leaf_moments_ref),
            preferred_element_type=jnp.float32,
        )
        spread = jnp.dot(
            transfer_ref[i], parent_field_ref[i // STRIP], preferred_element_type=jnp.float32
        )
        field_ref[i] = (field + spread).astype(jnp.bfloat16)

    tile_stage(0, 0)

    def pair_step(t, _):
        tile_stage(2 * t + 1, 1)
        sum_stage(2 * t, 0)
        tile_stage(jnp.minimum(2 * t + 2, leaves - 1), 0)
        sum_stage(2 * t + 1, 1)
        return 0

    lax.fori_loop(0, leaves // 2, pair_step, 0)

    share = leaves // NEAR_CALLS
    for part, near_ref in enumerate(near_refs):

        def last_step(k, _):
            i = part * share + k
            far = jnp.dot(basis_ref[i], field_ref[i], preferred_element_type=jnp.float32)
            out_ref[i] = jnp.transpose(near_ref[k] + far).astype(out_ref.dtype)
            return 0

        lax.fori_loop(0, share, last_step, 0, unroll=4)


def in_smem(count):
    return [pl.BlockSpec(memory_space=pltpu.SMEM)] * count


def in_vmem(count):
    return [pl.BlockSpec(memory_space=pltpu.VMEM)] * count


def per_device(
    points,
    charges,
    basis,
    transfer,
    leaf_skeleton,
    parent_skeleton,
    near_list,
    near_count,
    leaf_far,
    parent_far,
):
    rows_here, columns, leaf_count = charges.shape
    rank_size = basis.shape[1]
    near_index = lax.axis_index("near")
    leaf_index = lax.axis_index("leaf")
    rhs_index = lax.axis_index("rhs")
    rhs_parts = lax.axis_size("rhs")
    near_reach = 2 * STRIP + 2
    far_reach = 6 * STRIP - 1
    own = leaf_count // rhs_parts
    own_parents = own // STRIP
    own_start = rhs_index * own
    first_leaf = leaf_index * leaf_count + own_start
    all_columns = columns * rhs_parts

    def mine(array, dim, width=own, start=own_start):
        return lax.dynamic_slice_in_dim(array, start, width, dim)

    leaf_parts = lax.axis_size("leaf")
    near_parts = lax.axis_size("near")
    window = own + 2 * near_reach

    cells = jnp.transpose(charges, (2, 1, 0))

    def around(share):
        both = paired(share, rhs_index, 1)
        return mine(padded(both, "leaf", near_reach), 0, window)

    others = [rotated(cells, "near", k) for k in range(1, near_parts)]
    wide = around(cells)
    shares = [wide] + [around(share) for share in others]

    point_cells = jnp.transpose(points, (2, 0, 1))
    border_points = mine(padded(point_cells, "leaf", near_reach), 0, window)
    twice = jnp.concatenate([border_points, border_points], axis=2).astype(jnp.float32)
    border_points = mine(twice, 2, point_cells.shape[2], near_index * rows_here)
    own_points = border_points[near_reach : near_reach + own, :, :rows_here]

    listing = mine(near_list, 1)
    counts = mine(near_count, 0)
    row_ids = first_leaf + jnp.arange(own, dtype=jnp.int32)
    live = jnp.arange(near_list.shape[0], dtype=jnp.int32)[:, None] < counts[None, :]
    offset = (
        (listing % STRIP - row_ids[None, :] % STRIP + 2)
        + 5 * (listing // STRIP - row_ids[None, :] // STRIP + 2)
    )
    share = own // NEAR_CALLS
    idle = jnp.arange(own, dtype=jnp.int32) // share * share * 32 + 25
    code = jnp.where(live, (listing - (first_leaf - near_reach)) * 32 + offset, idle[None, :])
    slots = -(-near_list.shape[0] // GROUP) * GROUP
    spare = jnp.broadcast_to(idle[:, None], (own, slots - near_list.shape[0]))
    code = jnp.concatenate([jnp.transpose(code), spare], axis=1).reshape(-1)
    groups = (counts + (GROUP - 1)) // GROUP
    factor, added = offset_tables(border_points.shape[2])

    def near_call(part, after):
        share = own // NEAR_CALLS
        first = part * share
        cut = lambda array, start, width: lax.slice_in_dim(array, start, start + width, axis=0)
        part_codes = jnp.concatenate(
            [
                cut(code, first * slots, share * slots),
                jnp.full((slots,), first * 32 + 25, jnp.int32),
            ]
        )
        part_groups, after = lax.optimization_barrier((cut(groups, first, share), after))
        field = pl.pallas_call(
            functools.partial(near_kernel, slots, near_parts, first, share + 2 * near_reach),
            out_shape=jax.ShapeDtypeStruct((share, rows_here, all_columns), jnp.float32),
            in_specs=in_smem(2) + in_vmem(4 + near_parts),
            out_specs=pl.BlockSpec(memory_space=pltpu.VMEM),
            scratch_shapes=[
                pltpu.VMEM((window, FEATURES, border_points.shape[2]), jnp.bfloat16),
                pltpu.VMEM((share, rows_here, FEATURES), jnp.bfloat16),
                pltpu.VMEM((2, rows_here, GROUP * border_points.shape[2]), jnp.bfloat16),
                pltpu.SMEM((share * (slots // GROUP) + 3,), jnp.int32),
                pltpu.SMEM((share * (slots // GROUP) + 3,), jnp.int32),
            ],
            compiler_params=pltpu.CompilerParams(vmem_limit_bytes=48 * 2**20),
            cost_estimate=pl.CostEstimate(
                flops=30 * 10**9, bytes_accessed=16 * 10**6, transcendentals=0
            ),
            name="near_field",
        )(part_codes, part_groups, cut(own_points, first, share), border_points, factor, added, *shares)
        return field, after

    basis_cells = jnp.transpose(mine(basis, 2), (2, 0, 1))
    own_charges = lax.slice_in_dim(wide, near_reach, near_reach + own, axis=0)
    partial = jnp.einsum(
        "isa,ics->iac", basis_cells, own_charges, preferred_element_type=jnp.float32
    )
    sent = partial.astype(jnp.bfloat16)
    arrived = [rotated(sent, "near", k) for k in range(1, near_parts)]
    near_first, partial = near_call(0, partial)
    near_first, arrived = lax.optimization_barrier((near_first, arrived))
    for other in arrived:
        partial = partial + other.astype(jnp.float32)
    moments0 = partial.astype(jnp.bfloat16)
    transfer_cells = jnp.transpose(mine(transfer, 2), (2, 0, 1))
    moments1 = jnp.einsum(
        "pkb,pkc->pbc",
        transfer_cells.reshape(own_parents, STRIP * rank_size, rank_size),
        moments0.reshape(own_parents, STRIP * rank_size, all_columns),
        preferred_element_type=jnp.float32,
    ).astype(jnp.bfloat16)
    chip_parents = paired(moments1, rhs_index, 0)
    turned = lambda cells: [cells] + [rotated(cells, "leaf", k) for k in range(1, leaf_parts)]
    every_moments = turned(chip_parents)
    chip_moments = paired(moments0, rhs_index, 0)
    border_moments = halo(chip_moments, "leaf", far_reach)
    near_second, chip_moments = near_call(1, chip_moments)
    near_second, every_moments, border_moments = lax.optimization_barrier(
        (near_second, every_moments, border_moments)
    )
    every_moments = jnp.concatenate(every_moments, axis=0)
    border_moments = mine(jnp.concatenate(border_moments, axis=0), 0, own + 2 * far_reach)

    skeleton_cells = jnp.transpose(leaf_skeleton, (2, 0, 1))
    border_skeleton = mine(padded(skeleton_cells, "leaf", far_reach), 0, own + 2 * far_reach)
    parent_cells = jnp.transpose(parent_skeleton, (2, 0, 1))
    every_skeleton = jnp.concatenate(turned(parent_cells), axis=0)
    parent_start = rhs_index * own_parents
    leaf_ids = jnp.transpose(mine(leaf_far, 1) - (first_leaf - far_reach)).reshape(-1)
    chip_count = parent_far.shape[1]
    parent_ids = jnp.transpose(mine(parent_far, 1, own_parents, parent_start)).reshape(-1)
    parent_ids = (parent_ids + (leaf_parts - leaf_index) * chip_count) % (leaf_parts * chip_count)

    result = pl.pallas_call(
        functools.partial(far_kernel, leaf_far.shape[0], parent_far.shape[0], far_reach),
        out_shape=jax.ShapeDtypeStruct((own, all_columns, rows_here), jnp.bfloat16),
        in_specs=in_smem(3) + in_vmem(6 + NEAR_CALLS),
        out_specs=pl.BlockSpec(memory_space=pltpu.VMEM),
        scratch_shapes=[
            pltpu.VMEM((own + 2 * far_reach, rank_size, FEATURES), jnp.bfloat16),
            pltpu.VMEM((leaf_parts * chip_count, rank_size, FEATURES), jnp.bfloat16),
            pltpu.VMEM((own, rank_size, FEATURES), jnp.bfloat16),
            pltpu.VMEM((2, rank_size, leaf_far.shape[0] * rank_size), jnp.bfloat16),
            pltpu.VMEM((own_parents, rank_size, all_columns), jnp.bfloat16),
            pltpu.VMEM((own, rank_size, all_columns), jnp.bfloat16),
        ],
        compiler_params=pltpu.CompilerParams(vmem_limit_bytes=48 * 2**20),
        name="far_field",
    )(
        leaf_ids,
        parent_ids,
        parent_start.astype(jnp.int32).reshape(1),
        border_skeleton.astype(jnp.float32),
        border_moments,
        every_skeleton.astype(jnp.float32),
        every_moments,
        transfer_cells,
        basis_cells,
        near_first,
        near_second,
    )
    kept = mine(result, 1, columns, rhs_index * columns)
    given = mine(result, 1, columns, (1 - rhs_index) * columns)
    taken = rotated(given, "rhs", 1)
    first = rhs_index == 0
    result = jnp.concatenate(
        [jnp.where(first, kept, taken), jnp.where(first, taken, kept)], axis=0
    )
    return jnp.transpose(result, (2, 1, 0))


def solution(mesh):
    placed = (
        P(None, None, ("groups", "leaf")),
        P("near", "rhs", ("groups", "leaf")),
        P("near", None, ("groups", "leaf")),
        P(None, None, ("groups", "leaf")),
        P(None, None, ("groups", "leaf")),
        P(None, None, ("groups", "leaf")),
        P(None, ("groups", "leaf")),
        P(("groups", "leaf")),
        P(None, ("groups", "leaf")),
        P(None, ("groups", "leaf")),
    )
    return jax.shard_map(
        per_device,
        mesh=mesh,
        in_specs=placed,
        out_specs=P("near", "rhs", ("groups", "leaf")),
        check_vma=False,
    )
```
